32 devices in a mesh: slab: 8 (over z, y), thick: 4 (over x, core).
Axes of the slice: x: 2, y: 2, z: 4, core: 2. Of those that a mesh axis runs over, the one named last changes fastest.
Arguments:
- ref_pos: float32 [3, 524288], P(None, ('slab', 'thick')), may hold values from 0 to 8
- displacement: float32 [3, 524288], P(None, ('slab', 'thick')), may hold values from -1 to 1
- weighted_volume: float32 [524288], P(('slab', 'thick')), may hold values from 10 to 100
- ghost_corner_lists: int32 [2, 2, 512], P(None, None, ('slab', 'thick')), may hold values from 0 to 127
- bond_row_tiles: int32 [4096], P(('slab', 'thick')), may hold values from 0 to 127
- bond_column_tiles: int32 [4096], P(('slab', 'thick')), may hold values from 0 to 319, as said below
- bond_count: int32 [32], P(('slab', 'thick')), may hold values from 32 to 128, as said below
- bond_masks: int32 [4096, 16, 128], P(('slab', 'thick')), may hold values from 0 to 255
- broken_bonds: int32 [4096, 16, 128], P(('slab', 'thick')), may hold values from 0 to 255
Outputs:
- force: float32 [3, 524288], P(None, ('slab', 'thick'))
- dilatation: float32 [524288], P(('slab', 'thick'))
The draws below stay inside these ranges and needn't reach their ends.
Inputs may be any that keep to these rules, and one draw needn't show every extreme that they name: `bond_column_tiles`: an entry c below 128 names an owned tile; an entry at or above it names cycle cell (c - 128) // 16, only of neighbours that exist. `bond_count`: some device has exactly 128 live slots in every draw; live slots come first.
All inputs are finite; a program needn't handle non-finite values.
Results may differ from the reference program's by a relative error of at most 0.00015.
Values sent between devices are 32-bit elements; how exact they have to be, the bound alone decides.
A program may use at most 64 MiB of HBM per device.

```python
import math
import jax
import jax.numpy as jnp
from jax import lax

TILES_DEV = 128
GHOST = 16
BOND_TILES = 128
POINTS = 524288
SLOTS = 4096
LISTS = 512
N_SLAB = 8
N_THICK = 4
DEVICES = 32


def draw_bond_column_tiles(key, part):
    total = DEVICES * BOND_TILES
    keys = jax.random.split(key, 4)
    device_ids = jnp.arange(total, dtype=jnp.int32) // BOND_TILES
    slab_pos = device_ids // N_THICK
    thick_pos = device_ids % N_THICK
    cycle_table = jnp.array([0, 1, 2, 3, 4, 7, 8, 11, 12, 13, 14, 15], dtype=jnp.int32)
    cycle_cell = jax.random.randint(keys[0], (total,), 0, 12)
    position = cycle_table[cycle_cell]
    row_cell = position // 4
    col_cell = position % 4
    slab_step = jnp.where(row_cell == 0, -1, jnp.where(row_cell == 3, 1, 0))
    thick_step = jnp.where(col_cell == 0, -1, jnp.where(col_cell == 3, 1, 0))
    exists = (slab_pos + slab_step >= 0) & (slab_pos + slab_step < N_SLAB) & (thick_pos + thick_step >= 0) & (thick_pos + thick_step < N_THICK)
    choose_ghost = jax.random.randint(keys[1], (total,), 0, 2) == 1
    member = jax.random.randint(keys[2], (total,), 0, GHOST)
    owned = jax.random.randint(keys[3], (total,), 0, TILES_DEV)
    return jnp.where(exists & choose_ghost, TILES_DEV + cycle_cell * GHOST + member, owned).astype(jnp.int32)


def draw_bond_count(key, part):
    keys = jax.random.split(key, 2)
    counts = jax.random.randint(keys[0], (DEVICES,), BOND_TILES // 4, BOND_TILES + 1)
    busiest = jax.random.randint(keys[1], (), 0, DEVICES)
    return jnp.where(jnp.arange(DEVICES) == busiest, BOND_TILES, counts).astype(jnp.int32)


def with_ends(drawn, own_key, least, high):
    longest = drawn.shape.index(max(drawn.shape))
    spots = []
    for shift in (0, 1):
        where = [jax.random.randint(jax.random.fold_in(own_key, axis), (), 0, length) for axis, length in enumerate(drawn.shape)]
        where[longest] = (where[longest] + shift) % drawn.shape[longest]
        spots.append(tuple(where))
    return drawn.at[spots[0]].set(least).at[spots[1]].set(high)


def level_of(rng, dims, shards, least, largest):
    level = 1.0
    for dim, blocks in shards:
        heights = jax.random.uniform(jax.random.fold_in(jax.random.fold_in(rng, 6), dim), (blocks,), jnp.float32, least / len(shards), largest / len(shards))
        level = level * jnp.repeat(jnp.exp(heights), dims[dim] // blocks).reshape((-1,) + (1,) * (len(dims) - 1 - dim))
    return level


def normal_values(key, dims, scale, bound, cuts=(), held_as=jnp.bfloat16):
    drawn = jax.random.normal(key, dims, jnp.float32) * scale
    if len(cuts) > 0:
        drawn = level_of(key, dims, cuts, -0.22, 0.18) * drawn
    return jnp.clip(drawn, min=-bound, max=bound).astype(held_as)


def setup_inputs(seed: int = 0) -> dict:
    arg_keys = jax.random.split(jax.random.key(seed), 10)
    return {
        "ref_pos": jnp.clip(8.0 * jax.random.uniform(arg_keys[0], (3, POINTS), jnp.float32) ** level_of(arg_keys[0], (3, POINTS), ((1, 32),), -0.2, 0.2), 0.0, 8.0),
        "displacement": normal_values(arg_keys[1], (3, POINTS), 0.2, 1.0, ((1, 32),), jnp.float32),
        "weighted_volume": jnp.clip(jnp.exp(math.log(100.0) - 2.3025851 * jax.random.uniform(arg_keys[2], (POINTS,), jnp.float32) ** level_of(arg_keys[2], (POINTS,), ((0, 32),), -0.2, 0.2)), 10.0, 100.0),
        "ghost_corner_lists": with_ends(jax.random.randint(arg_keys[3], (2, 2, LISTS), 0, TILES_DEV), jax.random.fold_in(arg_keys[3], 1), 0, TILES_DEV - 1).astype(jnp.int32),
        "bond_row_tiles": with_ends(jax.random.randint(arg_keys[4], (SLOTS,), 0, TILES_DEV), jax.random.fold_in(arg_keys[4], 1), 0, TILES_DEV - 1).astype(jnp.int32),
        "bond_column_tiles": draw_bond_column_tiles(jax.random.fold_in(arg_keys[9], 71), 0),
        "bond_count": draw_bond_count(jax.random.fold_in(arg_keys[9], 71), 0),
        "bond_masks": with_ends(jax.random.randint(arg_keys[7], (SLOTS, 16, 128), 0, 256), jax.random.fold_in(arg_keys[7], 1), 0, 255).astype(jnp.int32),
        "broken_bonds": with_ends(jax.random.randint(arg_keys[8], (SLOTS, 16, 128), 0, 256), jax.random.fold_in(arg_keys[8], 1), 0, 255).astype(jnp.int32),
    }


young = 25.0
poisson = 0.22
bulk_modulus = young / (3.0 * (1.0 - 2.0 * poisson))
shear_modulus = young / (2.0 * (1.0 + poisson))
volumetric_term = 3.0 * bulk_modulus - 5.0 * shear_modulus
shear_term = 15.0 * shear_modulus
radius_floor = 0.5
cycle_cells = (0, 1, 2, 3, 4, 7, 8, 11, 12, 13, 14, 15)

def unpack_words(packed):
    shifts = jnp.arange(8, dtype=jnp.int32)
    spread = jnp.right_shift(packed[:, :, None, :], shifts[None, None, :, None]) & 1
    return spread.reshape(packed.shape[0], 128, 128).astype(jnp.float32)

def bond_geometry(row_payload, column_payload, packed_mask_words, fractured_bit_words, own_tile_list, active_slot_flags):
    ref_vec = column_payload[0:3, :, None, :] - row_payload[0:3, :, :, None]
    cur_vec = ref_vec + (column_payload[3:6, :, None, :] - row_payload[3:6, :, :, None])
    ref_len = jnp.maximum(jnp.sqrt(lax.optimization_barrier(jnp.sum(ref_vec * ref_vec, axis=0))), radius_floor)
    cur_len = jnp.maximum(jnp.sqrt(lax.optimization_barrier(jnp.sum(cur_vec * cur_vec, axis=0))), radius_floor)
    stretch = cur_len - ref_len
    below_diag = jnp.arange(128)[:, None] < jnp.arange(128)[None, :]
    keep_pair = jnp.where(own_tile_list[:, None, None], below_diag[None], True) & active_slot_flags[:, None, None]
    unbroken_flags = unpack_words(packed_mask_words) * (1.0 - unpack_words(fractured_bit_words)) * keep_pair.astype(jnp.float32)
    return (unbroken_flags, ref_len, cur_len, stretch, cur_vec)

def stretch_terms(row_payload, column_payload, packed_mask_words, fractured_bit_words, own_tile_list, active_slot_flags):
    unbroken_flags, ref_len, cur_len, stretch, cur_vec = bond_geometry(row_payload, column_payload, packed_mask_words, fractured_bit_words, own_tile_list, active_slot_flags)
    weighted = unbroken_flags * stretch
    return (lax.optimization_barrier(jnp.sum(weighted, axis=2)), lax.optimization_barrier(jnp.sum(weighted, axis=1)))

def force_contributions(row_payload, column_payload, packed_mask_words, fractured_bit_words, own_tile_list, active_slot_flags, row_dilatation, column_dilatation):
    unbroken_flags, ref_len, cur_len, stretch, cur_vec = bond_geometry(row_payload, column_payload, packed_mask_words, fractured_bit_words, own_tile_list, active_slot_flags)
    per_unit_length = shear_term * stretch / ref_len
    gathered_row = unbroken_flags * (volumetric_term * row_dilatation[:, :, None] + per_unit_length) / row_payload[6][:, :, None]
    gathered_column = unbroken_flags * (volumetric_term * column_dilatation[:, None, :] + per_unit_length) / column_payload[6][:, None, :]
    weight = (gathered_row + gathered_column) / cur_len
    pair_force = weight[None] * cur_vec
    return (lax.optimization_barrier(jnp.sum(pair_force, axis=3)), -lax.optimization_barrier(jnp.sum(pair_force, axis=2)))

def reference(ref_pos, displacement, weighted_volume, ghost_corner_lists, bond_row_tiles, bond_column_tiles, bond_count, bond_masks, broken_bonds):
    total_tiles = DEVICES * TILES_DEV
    point_state = jnp.concatenate([ref_pos, displacement, weighted_volume[None]], 0).reshape(7, total_tiles, 128)
    box_lists = ghost_corner_lists.reshape(2, 2, DEVICES, GHOST)
    device_ids = jnp.arange(DEVICES, dtype=jnp.int32)
    slab_pos = device_ids // N_THICK
    thick_pos = device_ids % N_THICK
    ghost_ids = []
    for cycle_cell in cycle_cells:
        row_cell = cycle_cell // 4
        col_cell = cycle_cell % 4
        slab_step = -1 if row_cell == 0 else 1 if row_cell == 3 else 0
        thick_step = -1 if col_cell == 0 else 1 if col_cell == 3 else 0
        slab_side = 1 if row_cell == 0 else 0 if row_cell == 3 else row_cell - 1
        thick_side = 1 if col_cell == 0 else 0 if col_cell == 3 else col_cell - 1
        near_slab = jnp.clip(slab_pos + slab_step, 0, N_SLAB - 1)
        near_thick = jnp.clip(thick_pos + thick_step, 0, N_THICK - 1)
        neighbour = (near_slab * N_THICK + near_thick).astype(jnp.int32)
        ghost_ids.append(neighbour[:, None] * TILES_DEV + box_lists[slab_side, thick_side][neighbour])
    ghost_table = jnp.stack(ghost_ids, 1).reshape(DEVICES, 12 * GHOST).astype(jnp.int32)
    rows_dev = bond_row_tiles.reshape(DEVICES, BOND_TILES)
    cols_dev = bond_column_tiles.reshape(DEVICES, BOND_TILES)
    ghost_slot = jnp.clip(cols_dev - TILES_DEV, 0, 12 * GHOST - 1).astype(jnp.int32)
    ghost_ref = jnp.take_along_axis(ghost_table, ghost_slot, axis=1)
    row_ids = (device_ids[:, None] * TILES_DEV + rows_dev).reshape(-1).astype(jnp.int32)
    col_ids = jnp.where(cols_dev < TILES_DEV, device_ids[:, None] * TILES_DEV + cols_dev, ghost_ref).reshape(-1).astype(jnp.int32)
    own_tile_list = (cols_dev == rows_dev).reshape(-1)
    active_slot_flags = (jnp.arange(BOND_TILES)[None, :] < bond_count[:, None]).reshape(-1)
    ref_width = 64
    block_total = DEVICES * BOND_TILES // ref_width

    def pieces(block_index):
        offset = block_index * ref_width
        ids_row = lax.dynamic_slice_in_dim(row_ids, offset, ref_width)
        ids_col = lax.dynamic_slice_in_dim(col_ids, offset, ref_width)
        return (ids_row, ids_col, jnp.take(point_state, ids_row, axis=1), jnp.take(point_state, ids_col, axis=1), lax.dynamic_slice_in_dim(bond_masks, offset, ref_width, 0), lax.dynamic_slice_in_dim(broken_bonds, offset, ref_width, 0), lax.dynamic_slice_in_dim(own_tile_list, offset, ref_width), lax.dynamic_slice_in_dim(active_slot_flags, offset, ref_width))

    def first_pass(block_index):
        ids_row, ids_col, row_payload, column_payload, masks_blk, broken_blk, self_blk, live_blk = pieces(block_index)
        return stretch_terms(row_payload, column_payload, masks_blk, broken_blk, self_blk, live_blk)
    row_terms, col_terms = lax.map(first_pass, jnp.arange(block_total, dtype=jnp.int32))
    stretch_sum = jax.ops.segment_sum(row_terms.reshape(-1, 128), row_ids, total_tiles) + jax.ops.segment_sum(col_terms.reshape(-1, 128), col_ids, total_tiles)
    dilatation = 3.0 * stretch_sum / point_state[6]

    def second_pass(block_index):
        ids_row, ids_col, row_payload, column_payload, masks_blk, broken_blk, self_blk, live_blk = pieces(block_index)
        return force_contributions(row_payload, column_payload, masks_blk, broken_blk, self_blk, live_blk, jnp.take(dilatation, ids_row, axis=0), jnp.take(dilatation, ids_col, axis=0))
    row_force, col_force = lax.map(second_pass, jnp.arange(block_total, dtype=jnp.int32))
    row_force = jnp.moveaxis(row_force, 1, 2).reshape(-1, 3, 128)
    col_force = jnp.moveaxis(col_force, 1, 2).reshape(-1, 3, 128)
    force_sum = jax.ops.segment_sum(row_force, row_ids, total_tiles) + jax.ops.segment_sum(col_force, col_ids, total_tiles)
    force = jnp.moveaxis(force_sum, 1, 0).reshape(3, total_tiles * 128)
    return (force, dilatation.reshape(total_tiles * 128))
```

```python
import functools

import jax
import jax.numpy as jnp
from jax import lax
from jax.experimental import pallas as pl
from jax.experimental.pallas import tpu as pltpu
from jax.sharding import PartitionSpec as P

young = 25.0
poisson = 0.22
bulk_modulus = young / (3.0 * (1.0 - 2.0 * poisson))
shear_modulus = young / (2.0 * (1.0 + poisson))
volumetric_term = 3.0 * bulk_modulus - 5.0 * shear_modulus
shear_term = 15.0 * shear_modulus
floor_squared = 0.25
centre = 4.0
cycle_cells = (0, 1, 2, 3, 4, 7, 8, 11, 12, 13, 14, 15)
MESH = pl.DeviceIdType.MESH
f32, bf16 = jnp.float32, jnp.bfloat16
UNROLL = 2
NN = (((1,), (0,)), ((), ()))
NT = (((1,), (1,)), ((), ()))
TN = (((0,), (0,)), ((), ()))


def cell_plan():
    plan = []
    for cell in cycle_cells:
        row, col = cell // 4, cell % 4
        step = (-1, 0, 0, 1)
        side = (1, 0, 1, 0)
        plan.append((step[row], step[col], 2 * side[row] + side[col]))
    return plan


def dot(a, b, dims):
    return lax.dot_general(a, b, dims, preferred_element_type=f32)


def rounded(x):
    return x.astype(bf16).astype(f32)


def split3(x):
    high = rounded(x)
    rest = x - high
    middle = rounded(rest)
    return high, middle, rest - middle


def split2(x):
    high = x.astype(bf16)
    return high, (x - high.astype(f32)).astype(bf16)


def hot_dot(hot, x):
    high, middle, low = split3(x)
    return (
        dot(hot, high.astype(bf16), NN)
        + dot(hot, middle.astype(bf16), NN)
        + dot(hot, low.astype(bf16), NN)
    )


def features(payload):
    row = lax.broadcasted_iota(jnp.int32, payload.shape, 0)
    high, middle, low = split3(payload)
    square = payload * payload
    cur = jnp.sum(square[0:3], axis=0, keepdims=True)
    ref = jnp.sum(square[4:7], axis=0, keepdims=True)
    norm = jnp.where(row < 4, cur, ref)
    n_high, n_middle, n_low = split3(norm)
    which = row & 3
    norms = jnp.where(
        which == 0, n_high, jnp.where(which == 1, n_middle, jnp.where(which == 2, n_low, 0.0))
    )
    return high, middle, low, norms


def weighted_rows(payload, scale):
    row = lax.broadcasted_iota(jnp.int32, payload.shape, 0)
    both = jnp.where(row < 4, payload, scale * pltpu.roll(payload, 4, 0))
    pieces = jnp.concatenate(split3(both), axis=0).astype(bf16)
    return jnp.concatenate([pieces, pieces], axis=1)


def fold(stacked, scale):
    total = stacked[0:8] + stacked[8:16] + stacked[16:24]
    return scale * total + pltpu.roll(total, 4, 0)


def kernel(
    axes,
    row_ref,
    col_ref,
    count_ref,
    list_ref,
    row_vec,
    col_vec,
    list_vec,
    pos_ref,
    disp_ref,
    vol_ref,
    mask_ref,
    broken_ref,
    force_ref,
    dil_ref,
    tab,
    out_buf,
    ghost_in,
    row_sum,
    col_sum,
    sum_out,
    sum_in,
    alpha_tab,
    alpha_out,
    alpha_in,
    p_high,
    p_low,
    q_row,
    q_col,
    row_force,
    col_force,
    force_out,
    force_in,
    send_sem,
    recv_sem,
):
    slab, thick = axes
    si, ti = lax.axis_index(slab), lax.axis_index(thick)
    n_slab, n_thick = lax.axis_size(slab), lax.axis_size(thick)
    tiles = vol_ref.shape[0]
    slots = row_vec.shape[1]
    g = list_vec.shape[1] // 4
    plan = cell_plan()

    def there(ds, dt):
        s, t = si + ds, ti + dt
        return (s >= 0) & (s < n_slab) & (t >= 0) & (t < n_thick)

    steps = [(a, b) for a in (-1, 0, 1) for b in (-1, 0, 1) if (a, b) != (0, 0)]
    barrier = pltpu.get_barrier_semaphore()
    for ds, dt in steps:

        @pl.when(there(ds, dt))
        def _(ds=ds, dt=dt):
            pl.semaphore_signal(barrier, inc=1, device_id=(si + ds, ti + dt), device_id_type=MESH)

    def copy_of(phase, q, source, target, ds, dt):
        return pltpu.make_async_remote_copy(
            src_ref=source(q),
            dst_ref=target(q),
            send_sem=send_sem.at[phase, q],
            recv_sem=recv_sem.at[phase, q],
            device_id=(si + ds, ti + dt),
            device_id_type=MESH,
        )

    def exchange(phase, source, target, sign):
        for q, (ds, dt, _c) in enumerate(plan):

            @pl.when(there(sign * ds, sign * dt))
            def _(q=q, ds=sign * ds, dt=sign * dt):
                copy_of(phase, q, source, target, ds, dt).start()

    def finish(phase, source, target, sign):
        for q, (ds, dt, _c) in enumerate(plan):

            @pl.when(there(-sign * ds, -sign * dt))
            def _(q=q, ds=-sign * ds, dt=-sign * dt):
                copy_of(phase, q, source, target, ds, dt).wait_recv()

            @pl.when(there(sign * ds, sign * dt))
            def _(q=q, ds=sign * ds, dt=sign * dt):
                copy_of(phase, q, source, target, ds, dt).wait_send()

    for q, (ds, dt, _c) in enumerate(plan):

        @pl.when(jnp.logical_not(there(ds, dt)))
        def _(q=q):
            ghost_in[q * g : (q + 1) * g] = jnp.zeros((g, 8, 128), f32)
            alpha_in[q * g : (q + 1) * g] = jnp.zeros((g, 128), f32)

        @pl.when(jnp.logical_not(there(-ds, -dt)))
        def _(q=q):
            sum_in[q] = jnp.zeros((g, 128), f32)
            force_in[q] = jnp.zeros((g, 384), f32)

    def build(t, carry):
        at = pl.ds(pl.multiple_of(t * 128, 128), 128)
        ref = pos_ref[:, at] - centre
        tab[t] = jnp.concatenate(
            [
                ref + disp_ref[:, at],
                jnp.ones((1, 128), f32),
                ref,
                shear_term / vol_ref[pl.ds(t, 1), :],
            ],
            axis=0,
        )
        return carry

    lax.fori_loop(0, tiles, build, 0, unroll=4)

    for s in range(2):
        for t in range(2):

            def pick(i, carry, s=s, t=t):
                out_buf[(2 * s + t) * g + i] = tab[list_ref[s, t, i]]
                return carry

            lax.fori_loop(0, g, pick, 0, unroll=4)

    peers = sum(there(ds, dt).astype(jnp.int32) for ds, dt in steps)
    pl.semaphore_wait(barrier, peers)

    corner = [c for _s, _t, c in plan]
    payload = (
        0,
        lambda q: out_buf.at[corner[q] * g : (corner[q] + 1) * g],
        lambda q: ghost_in.at[q * g : (q + 1) * g],
        -1,
    )
    exchange(*payload)
    finish(*payload)
    tab[tiles:] = ghost_in[...]

    sub = lax.broadcasted_iota(jnp.int32, (8, 128), 0)
    cur_rows = (sub < 3).astype(f32)
    ref_rows = ((sub >= 4) & (sub < 7)).astype(f32)
    one8 = jnp.ones((8, 128), f32)
    ones = jnp.ones((8, 256), bf16)
    word = lax.broadcasted_iota(jnp.int32, (16, 128), 0)
    lane = lax.broadcasted_iota(jnp.int32, (16, 128), 1)
    triangle = (1 << jnp.clip(lane - 8 * word, 0, 8)) - 1
    bit = lax.broadcasted_iota(jnp.int32, (16, 8, 128), 1)
    live = count_ref[0]

    def first(k):
        a, b = row_ref[k], col_ref[k]
        vi, vj = tab[a], tab[b]
        hi, mi, li, ni = features(vi)
        hj, mj, lj, nj = features(vj)
        left = jnp.concatenate([hi, hi, mi, mi, hi, li, ni, one8], axis=0).astype(bf16)
        hj, mj, lj = -2.0 * hj, -2.0 * mj, -2.0 * lj
        base = (hj, mj, hj, mj, lj, hj, one8, nj)
        right = jnp.concatenate(
            [
                jnp.concatenate([x * ref_rows for x in base], axis=0),
                jnp.concatenate([x * cur_rows for x in base], axis=0),
            ],
            axis=1,
        ).astype(bf16)
        squares = jnp.maximum(dot(left, right, TN), floor_squared)
        ref_sq, cur_sq = squares[:, 0:128], squares[:, 128:256]
        ref_inv, cur_inv = lax.rsqrt(ref_sq), lax.rsqrt(cur_sq)
        words = mask_ref[k] & ~broken_ref[k]
        words = words & jnp.where(a == b, triangle, 255)
        words = words & jnp.where(k < live, 255, 0)
        spread = jnp.broadcast_to(words[:, None, :], (16, 8, 128))
        keep = ((spread & (1 << bit)) != 0).reshape(128, 128)
        e = jnp.where(keep, cur_sq * cur_inv - ref_sq * ref_inv, 0.0)
        p = jnp.where(keep, cur_inv, 0.0)
        q = jnp.where(keep, ref_inv - cur_inv, 0.0)
        col_sum[pl.ds(k, 1), :] = jnp.sum(e, axis=0, keepdims=True)
        row_sum[pl.ds(k, 1), :] = dot(ones, jnp.concatenate(split2(e), axis=1), NT)[0:1]
        ph, plow = split2(p)
        p_high[k] = ph
        p_low[k] = plow
        qh, qlow = split2(q)
        gi, gj = vi[7:8], vj[7:8]
        q_row[k] = fold(
            dot(weighted_rows(vj, gj), jnp.concatenate([qh, qlow], axis=1), NT), gi
        )
        q_col[k] = fold(
            dot(weighted_rows(vi, gi), jnp.concatenate([qh, qlow], axis=0), NN), gj
        )

    def first_loop(block, carry):
        for u in range(UNROLL):
            first(block * UNROLL + u)
        return carry

    lax.fori_loop(0, slots // UNROLL, first_loop, 0)

    row_hot = (
        lax.broadcasted_iota(jnp.int32, (tiles, slots), 0) == row_vec[...]
    ).astype(f32).astype(bf16)
    col_hot = (
        lax.broadcasted_iota(jnp.int32, (tiles + 12 * g, slots), 0) == col_vec[...]
    ).astype(f32).astype(bf16)
    box_hot = (
        lax.broadcasted_iota(jnp.int32, (tiles, 4 * g), 0) == list_vec[...]
    ).astype(f32).astype(bf16)

    def returned(buffer):
        corners = []
        for c in range(4):
            parts = [buffer[q] for q in range(12) if corner[q] == c]
            corners.append(parts[0] + parts[1] + parts[2])
        return hot_dot(box_hot, jnp.concatenate(corners, axis=0))

    col_part = hot_dot(col_hot, col_sum[...])
    sum_out[...] = col_part[tiles:]
    sums = (1, lambda q: sum_out.at[q * g : (q + 1) * g], lambda q: sum_in.at[q], 1)
    exchange(*sums)
    own = hot_dot(row_hot, row_sum[...]) + col_part[:tiles]
    finish(*sums)
    volume = vol_ref[...]
    dilatation = 3.0 * (own + returned(sum_in)) / volume
    dil_ref[...] = dilatation
    alpha_tab[0:tiles] = volumetric_term * dilatation / volume

    for s in range(2):
        for t in range(2):

            def pick_alpha(i, carry, s=s, t=t):
                alpha_out[pl.ds((2 * s + t) * g + i, 1), :] = alpha_tab[
                    pl.ds(list_ref[s, t, i], 1), :
                ]
                return carry

            lax.fori_loop(0, g, pick_alpha, 0, unroll=4)

    alphas = (
        2,
        lambda q: alpha_out.at[corner[q] * g : (corner[q] + 1) * g],
        lambda q: alpha_in.at[q * g : (q + 1) * g],
        -1,
    )
    exchange(*alphas)
    finish(*alphas)
    alpha_tab[tiles:] = alpha_in[...]

    def second(k):
        a, b = row_ref[k], col_ref[k]
        vi, vj = tab[a], tab[b]
        ai, aj = alpha_tab[pl.ds(a, 1), :], alpha_tab[pl.ds(b, 1), :]
        ph, plow = p_high[k], p_low[k]
        rows = q_row[k] + fold(
            dot(weighted_rows(vj, aj), jnp.concatenate([ph, plow], axis=1), NT), ai
        )
        cols = q_col[k] + fold(
            dot(weighted_rows(vi, ai), jnp.concatenate([ph, plow], axis=0), NN), aj
        )
        rows = rows - vi * rows[3:4]
        cols = cols - vj * cols[3:4]
        for c in range(3):
            row_force[c, pl.ds(k, 1), :] = rows[c : c + 1]
            col_force[c, pl.ds(k, 1), :] = cols[c : c + 1]

    def second_loop(block, carry):
        for u in range(UNROLL):
            second(block * UNROLL + u)
        return carry

    lax.fori_loop(0, slots // UNROLL, second_loop, 0)

    col_part = hot_dot(col_hot, jnp.concatenate([col_force[c] for c in range(3)], axis=1))
    force_out[...] = col_part[tiles:]
    forces = (3, lambda q: force_out.at[q * g : (q + 1) * g], lambda q: force_in.at[q], 1)
    exchange(*forces)
    own = hot_dot(row_hot, jnp.concatenate([row_force[c] for c in range(3)], axis=1)) + col_part[:tiles]
    finish(*forces)
    total = own + returned(force_in)
    for c in range(3):
        force_ref[c] = total[:, c * 128 : (c + 1) * 128]


def body(
    ref_pos,
    displacement,
    weighted_volume,
    ghost_corner_lists,
    bond_row_tiles,
    bond_column_tiles,
    bond_count,
    bond_masks,
    broken_bonds,
):
    points = ref_pos.shape[1]
    tiles = points // 128
    g = ghost_corner_lists.shape[2]
    slots = bond_row_tiles.shape[0]
    smem = pl.BlockSpec(memory_space=pltpu.SMEM)
    vmem = pl.BlockSpec(memory_space=pltpu.VMEM)
    force, dilatation = pl.pallas_call(
        functools.partial(kernel, ("slab", "thick")),
        out_shape=(
            jax.ShapeDtypeStruct((3, tiles, 128), f32),
            jax.ShapeDtypeStruct((tiles, 128), f32),
        ),
        in_specs=[smem] * 4 + [vmem] * 8,
        out_specs=(vmem, vmem),
        scratch_shapes=[
            pltpu.VMEM((tiles + 12 * g, 8, 128), f32),
            pltpu.VMEM((4 * g, 8, 128), f32),
            pltpu.VMEM((12 * g, 8, 128), f32),
            pltpu.VMEM((slots, 128), f32),
            pltpu.VMEM((slots, 128), f32),
            pltpu.VMEM((12 * g, 128), f32),
            pltpu.VMEM((12, g, 128), f32),
            pltpu.VMEM((tiles + 12 * g, 128), f32),
            pltpu.VMEM((4 * g, 128), f32),
            pltpu.VMEM((12 * g, 128), f32),
            pltpu.VMEM((slots, 128, 128), bf16),
            pltpu.VMEM((slots, 128, 128), bf16),
            pltpu.VMEM((slots, 8, 128), f32),
            pltpu.VMEM((slots, 8, 128), f32),
            pltpu.VMEM((3, slots, 128), f32),
            pltpu.VMEM((3, slots, 128), f32),
            pltpu.VMEM((12 * g, 384), f32),
            pltpu.VMEM((12, g, 384), f32),
            pltpu.SemaphoreType.DMA((4, 12)),
            pltpu.SemaphoreType.DMA((4, 12)),
        ],
        compiler_params=pltpu.CompilerParams(
            collective_id=0, has_side_effects=True, vmem_limit_bytes=40 * 1024 * 1024
        ),
    )(
        bond_row_tiles,
        bond_column_tiles,
        bond_count,
        ghost_corner_lists,
        bond_row_tiles.reshape(1, slots),
        bond_column_tiles.reshape(1, slots),
        ghost_corner_lists.reshape(1, 4 * g),
        ref_pos,
        displacement,
        weighted_volume.reshape(tiles, 128),
        bond_masks,
        broken_bonds,
    )
    return force.reshape(3, points), dilatation.reshape(points)


def solution(mesh):
    in_specs = (
        P(None, ("slab", "thick")),
        P(None, ("slab", "thick")),
        P(("slab", "thick")),
        P(None, None, ("slab", "thick")),
        P(("slab", "thick")),
        P(("slab", "thick")),
        P(("slab", "thick")),
        P(("slab", "thick"), None, None),
        P(("slab", "thick"), None, None),
    )
    out_specs = (P(None, ("slab", "thick")), P(("slab", "thick")))
    return jax.shard_map(body, mesh=mesh, in_specs=in_specs, out_specs=out_specs, check_vma=False)
```

```python
import functools

import jax
import jax.numpy as jnp
from jax import lax
from jax.experimental import pallas as pl
from jax.experimental.pallas import tpu as pltpu
from jax.sharding import PartitionSpec as P

young = 25.0
poisson = 0.22
bulk_modulus = young / (3.0 * (1.0 - 2.0 * poisson))
shear_modulus = young / (2.0 * (1.0 + poisson))
volumetric_term = 3.0 * bulk_modulus - 5.0 * shear_modulus
shear_term = 15.0 * shear_modulus
floor_squared = 0.25
centre = 4.0
cycle_cells = (0, 1, 2, 3, 4, 7, 8, 11, 12, 13, 14, 15)
MESH = pl.DeviceIdType.MESH
f32, bf16 = jnp.float32, jnp.bfloat16
UNROLL = 4
NN = (((1,), (0,)), ((), ()))
NT = (((1,), (1,)), ((), ()))
TN = (((0,), (0,)), ((), ()))


def cell_plan():
    plan = []
    for cell in cycle_cells:
        row, col = cell // 4, cell % 4
        step = (-1, 0, 0, 1)
        side = (1, 0, 1, 0)
        plan.append((step[row], step[col], 2 * side[row] + side[col]))
    return plan


def dot(a, b, dims):
    return lax.dot_general(a, b, dims, preferred_element_type=f32)


def rounded(x):
    return x.astype(bf16).astype(f32)


def split3(x):
    high = rounded(x)
    rest = x - high
    middle = rounded(rest)
    return high, middle, rest - middle


def split2(x):
    high = x.astype(bf16)
    return high, (x - high.astype(f32)).astype(bf16)


def hot_dot(hot, x):
    high, middle, low = split3(x)
    return (
        dot(hot, high.astype(bf16), NN)
        + dot(hot, middle.astype(bf16), NN)
        + dot(hot, low.astype(bf16), NN)
    )


def features(payload):
    row = lax.broadcasted_iota(jnp.int32, payload.shape, 0)
    high, middle, low = split3(payload)
    square = payload * payload
    cur = jnp.sum(square[0:3], axis=0, keepdims=True)
    ref = jnp.sum(square[4:7], axis=0, keepdims=True)
    norm = jnp.where(row < 4, cur, ref)
    n_high, n_middle, n_low = split3(norm)
    which = row & 3
    norms = jnp.where(
        which == 0, n_high, jnp.where(which == 1, n_middle, jnp.where(which == 2, n_low, 0.0))
    )
    return high, middle, low, norms


def weighted_rows(payload, scale):
    row = lax.broadcasted_iota(jnp.int32, payload.shape, 0)
    both = jnp.where(row < 4, payload, scale * pltpu.roll(payload, 4, 0))
    pieces = jnp.concatenate(split3(both), axis=0).astype(bf16)
    return jnp.concatenate([pieces, pieces], axis=1)


def fold(stacked, scale):
    total = stacked[0:8] + stacked[8:16] + stacked[16:24]
    return scale * total + pltpu.roll(total, 4, 0)


def kernel(
    axes,
    row_ref,
    col_ref,
    count_ref,
    list_ref,
    row_vec,
    col_vec,
    list_vec,
    pos_ref,
    disp_ref,
    vol_ref,
    mask_hbm,
    broken_hbm,
    force_ref,
    dil_ref,
    mask_ref,
    broken_ref,
    tab,
    out_buf,
    ghost_in,
    row_sum,
    col_sum,
    sum_out,
    sum_in,
    alpha_tab,
    alpha_out,
    alpha_in,
    p_high,
    p_low,
    q_row,
    q_col,
    row_force,
    col_force,
    force_out,
    force_in,
    send_sem,
    recv_sem,
    load_sem,
):
    mask_load = pltpu.make_async_copy(mask_hbm, mask_ref, load_sem.at[0])
    broken_load = pltpu.make_async_copy(broken_hbm, broken_ref, load_sem.at[1])
    mask_load.start()
    broken_load.start()
    slab, thick = axes
    si, ti = lax.axis_index(slab), lax.axis_index(thick)
    n_slab, n_thick = lax.axis_size(slab), lax.axis_size(thick)
    tiles = vol_ref.shape[0]
    slots = row_vec.shape[1]
    g = list_vec.shape[1] // 4
    plan = cell_plan()

    def there(ds, dt):
        s, t = si + ds, ti + dt
        return (s >= 0) & (s < n_slab) & (t >= 0) & (t < n_thick)

    steps = [(a, b) for a in (-1, 0, 1) for b in (-1, 0, 1) if (a, b) != (0, 0)]
    barrier = pltpu.get_barrier_semaphore()
    for ds, dt in steps:

        @pl.when(there(ds, dt))
        def _(ds=ds, dt=dt):
            pl.semaphore_signal(barrier, inc=1, device_id=(si + ds, ti + dt), device_id_type=MESH)

    def copy_of(phase, q, source, target, ds, dt):
        return pltpu.make_async_remote_copy(
            src_ref=source(q),
            dst_ref=target(q),
            send_sem=send_sem.at[phase, q],
            recv_sem=recv_sem.at[phase, q],
            device_id=(si + ds, ti + dt),
            device_id_type=MESH,
        )

    def exchange(phase, source, target, sign):
        for q, (ds, dt, _c) in enumerate(plan):

            @pl.when(there(sign * ds, sign * dt))
            def _(q=q, ds=sign * ds, dt=sign * dt):
                copy_of(phase, q, source, target, ds, dt).start()

    def finish(phase, source, target, sign):
        for q, (ds, dt, _c) in enumerate(plan):

            @pl.when(there(-sign * ds, -sign * dt))
            def _(q=q, ds=-sign * ds, dt=-sign * dt):
                copy_of(phase, q, source, target, ds, dt).wait_recv()

            @pl.when(there(sign * ds, sign * dt))
            def _(q=q, ds=sign * ds, dt=sign * dt):
                copy_of(phase, q, source, target, ds, dt).wait_send()

    for q, (ds, dt, _c) in enumerate(plan):

        @pl.when(jnp.logical_not(there(ds, dt)))
        def _(q=q):
            ghost_in[q * g : (q + 1) * g] = jnp.zeros((g, 8, 128), f32)
            alpha_in[q * g : (q + 1) * g] = jnp.zeros((g, 128), f32)

        @pl.when(jnp.logical_not(there(-ds, -dt)))
        def _(q=q):
            sum_in[q] = jnp.zeros((g, 128), f32)
            force_in[q] = jnp.zeros((g, 384), f32)

    def build(t, carry):
        at = pl.ds(pl.multiple_of(t * 128, 128), 128)
        ref = pos_ref[:, at] - centre
        tab[t] = jnp.concatenate(
            [
                ref + disp_ref[:, at],
                jnp.ones((1, 128), f32),
                ref,
                shear_term / vol_ref[pl.ds(t, 1), :],
            ],
            axis=0,
        )
        return carry

    lax.fori_loop(0, tiles, build, 0, unroll=4)

    for s in range(2):
        for t in range(2):

            def pick(i, carry, s=s, t=t):
                out_buf[(2 * s + t) * g + i] = tab[list_ref[s, t, i]]
                return carry

            lax.fori_loop(0, g, pick, 0, unroll=4)

    peers = sum(there(ds, dt).astype(jnp.int32) for ds, dt in steps)
    pl.semaphore_wait(barrier, peers)

    corner = [c for _s, _t, c in plan]
    payload = (
        0,
        lambda q: out_buf.at[corner[q] * g : (corner[q] + 1) * g],
        lambda q: ghost_in.at[q * g : (q + 1) * g],
        -1,
    )
    exchange(*payload)
    finish(*payload)
    tab[tiles:] = ghost_in[...]
    mask_load.wait()
    broken_load.wait()

    sub = lax.broadcasted_iota(jnp.int32, (8, 128), 0)
    cur_rows = (sub < 3).astype(f32)
    ref_rows = ((sub >= 4) & (sub < 7)).astype(f32)
    one8 = jnp.ones((8, 128), f32)
    ones = jnp.ones((8, 256), bf16)
    word = lax.broadcasted_iota(jnp.int32, (16, 128), 0)
    lane = lax.broadcasted_iota(jnp.int32, (16, 128), 1)
    triangle = (1 << jnp.clip(lane - 8 * word, 0, 8)) - 1
    bit = lax.broadcasted_iota(jnp.int32, (16, 8, 128), 1)
    live = count_ref[0]

    def first(k):
        a, b = row_ref[k], col_ref[k]
        vi, vj = tab[a], tab[b]
        hi, mi, li, ni = features(vi)
        hj, mj, lj, nj = features(vj)
        left = jnp.concatenate([hi, hi, mi, mi, hi, li, ni, one8], axis=0).astype(bf16)
        hj, mj, lj = -2.0 * hj, -2.0 * mj, -2.0 * lj
        base = (hj, mj, hj, mj, lj, hj, one8, nj)
        right = jnp.concatenate(
            [
                jnp.concatenate([x * ref_rows for x in base], axis=0),
                jnp.concatenate([x * cur_rows for x in base], axis=0),
            ],
            axis=1,
        ).astype(bf16)
        squares = jnp.maximum(dot(left, right, TN), floor_squared)
        ref_sq, cur_sq = squares[:, 0:128], squares[:, 128:256]
        ref_inv, cur_inv = lax.rsqrt(ref_sq), lax.rsqrt(cur_sq)
        words = mask_ref[k] & ~broken_ref[k]
        words = words & jnp.where(a == b, triangle, 255)
        words = words & jnp.where(k < live, 255, 0)
        spread = jnp.broadcast_to(words[:, None, :], (16, 8, 128))
        keep = ((spread & (1 << bit)) != 0).reshape(128, 128)
        e = jnp.where(keep, cur_sq * cur_inv - ref_sq * ref_inv, 0.0)
        p = jnp.where(keep, cur_inv, 0.0)
        q = jnp.where(keep, ref_inv - cur_inv, 0.0)
        col_sum[pl.ds(k, 1), :] = jnp.sum(e, axis=0, keepdims=True)
        row_sum[pl.ds(k, 1), :] = dot(ones, jnp.concatenate(split2(e), axis=1), NT)[0:1]
        ph, plow = split2(p)
        p_high[k] = ph
        p_low[k] = plow
        qh, qlow = split2(q)
        gi, gj = vi[7:8], vj[7:8]
        q_row[k] = fold(
            dot(weighted_rows(vj, gj), jnp.concatenate([qh, qlow], axis=1), NT), gi
        )
        q_col[k] = fold(
            dot(weighted_rows(vi, gi), jnp.concatenate([qh, qlow], axis=0), NN), gj
        )

    def first_loop(block, carry):
        for u in range(UNROLL):
            first(block * UNROLL + u)
        return carry

    lax.fori_loop(0, slots // UNROLL, first_loop, 0)

    row_hot = (
        lax.broadcasted_iota(jnp.int32, (tiles, slots), 0) == row_vec[...]
    ).astype(f32).astype(bf16)
    col_hot = (
        lax.broadcasted_iota(jnp.int32, (tiles + 12 * g, slots), 0) == col_vec[...]
    ).astype(f32).astype(bf16)
    box_hot = (
        lax.broadcasted_iota(jnp.int32, (tiles, 4 * g), 0) == list_vec[...]
    ).astype(f32).astype(bf16)

    def returned(buffer):
        corners = []
        for c in range(4):
            parts = [buffer[q] for q in range(12) if corner[q] == c]
            corners.append(parts[0] + parts[1] + parts[2])
        return hot_dot(box_hot, jnp.concatenate(corners, axis=0))

    col_part = hot_dot(col_hot, col_sum[...])
    sum_out[...] = col_part[tiles:]
    sums = (1, lambda q: sum_out.at[q * g : (q + 1) * g], lambda q: sum_in.at[q], 1)
    exchange(*sums)
    own = hot_dot(row_hot, row_sum[...]) + col_part[:tiles]
    finish(*sums)
    volume = vol_ref[...]
    dilatation = 3.0 * (own + returned(sum_in)) / volume
    dil_ref[...] = dilatation
    alpha_tab[0:tiles] = volumetric_term * dilatation / volume

    for s in range(2):
        for t in range(2):

            def pick_alpha(i, carry, s=s, t=t):
                alpha_out[pl.ds((2 * s + t) * g + i, 1), :] = alpha_tab[
                    pl.ds(list_ref[s, t, i], 1), :
                ]
                return carry

            lax.fori_loop(0, g, pick_alpha, 0, unroll=4)

    alphas = (
        2,
        lambda q: alpha_out.at[corner[q] * g : (corner[q] + 1) * g],
        lambda q: alpha_in.at[q * g : (q + 1) * g],
        -1,
    )
    exchange(*alphas)
    finish(*alphas)
    alpha_tab[tiles:] = alpha_in[...]

    def second(k):
        a, b = row_ref[k], col_ref[k]
        vi, vj = tab[a], tab[b]
        ai, aj = alpha_tab[pl.ds(a, 1), :], alpha_tab[pl.ds(b, 1), :]
        ph, plow = p_high[k], p_low[k]
        rows = q_row[k] + fold(
            dot(weighted_rows(vj, aj), jnp.concatenate([ph, plow], axis=1), NT), ai
        )
        cols = q_col[k] + fold(
            dot(weighted_rows(vi, ai), jnp.concatenate([ph, plow], axis=0), NN), aj
        )
        rows = rows - vi * rows[3:4]
        cols = cols - vj * cols[3:4]
        for c in range(3):
            row_force[c, pl.ds(k, 1), :] = rows[c : c + 1]
            col_force[c, pl.ds(k, 1), :] = cols[c : c + 1]

    def second_loop(block, carry):
        for u in range(UNROLL):
            second(block * UNROLL + u)
        return carry

    lax.fori_loop(0, slots // UNROLL, second_loop, 0)

    col_part = hot_dot(col_hot, jnp.concatenate([col_force[c] for c in range(3)], axis=1))
    force_out[...] = col_part[tiles:]
    forces = (3, lambda q: force_out.at[q * g : (q + 1) * g], lambda q: force_in.at[q], 1)
    exchange(*forces)
    own = hot_dot(row_hot, jnp.concatenate([row_force[c] for c in range(3)], axis=1)) + col_part[:tiles]
    finish(*forces)
    total = own + returned(force_in)
    for c in range(3):
        force_ref[c] = total[:, c * 128 : (c + 1) * 128]


def body(
    ref_pos,
    displacement,
    weighted_volume,
    ghost_corner_lists,
    bond_row_tiles,
    bond_column_tiles,
    bond_count,
    bond_masks,
    broken_bonds,
):
    points = ref_pos.shape[1]
    tiles = points // 128
    g = ghost_corner_lists.shape[2]
    slots = bond_row_tiles.shape[0]
    smem = pl.BlockSpec(memory_space=pltpu.SMEM)
    vmem = pl.BlockSpec(memory_space=pltpu.VMEM)
    force, dilatation = pl.pallas_call(
        functools.partial(kernel, ("slab", "thick")),
        out_shape=(
            jax.ShapeDtypeStruct((3, tiles, 128), f32),
            jax.ShapeDtypeStruct((tiles, 128), f32),
        ),
        in_specs=[smem] * 4 + [vmem] * 6 + [pl.BlockSpec(memory_space=pl.ANY)] * 2,
        out_specs=(vmem, vmem),
        scratch_shapes=[
            pltpu.VMEM(bond_masks.shape, jnp.int32),
            pltpu.VMEM(bond_masks.shape, jnp.int32),
            pltpu.VMEM((tiles + 12 * g, 8, 128), f32),
            pltpu.VMEM((4 * g, 8, 128), f32),
            pltpu.VMEM((12 * g, 8, 128), f32),
            pltpu.VMEM((slots, 128), f32),
            pltpu.VMEM((slots, 128), f32),
            pltpu.VMEM((12 * g, 128), f32),
            pltpu.VMEM((12, g, 128), f32),
            pltpu.VMEM((tiles + 12 * g, 128), f32),
            pltpu.VMEM((4 * g, 128), f32),
            pltpu.VMEM((12 * g, 128), f32),
            pltpu.VMEM((slots, 128, 128), bf16),
            pltpu.VMEM((slots, 128, 128), bf16),
            pltpu.VMEM((slots, 8, 128), f32),
            pltpu.VMEM((slots, 8, 128), f32),
            pltpu.VMEM((3, slots, 128), f32),
            pltpu.VMEM((3, slots, 128), f32),
            pltpu.VMEM((12 * g, 384), f32),
            pltpu.VMEM((12, g, 384), f32),
            pltpu.SemaphoreType.DMA((4, 12)),
            pltpu.SemaphoreType.DMA((4, 12)),
            pltpu.SemaphoreType.DMA((2,)),
        ],
        compiler_params=pltpu.CompilerParams(
            collective_id=0, has_side_effects=True, vmem_limit_bytes=40 * 1024 * 1024
        ),
    )(
        bond_row_tiles,
        bond_column_tiles,
        bond_count,
        ghost_corner_lists,
        bond_row_tiles.reshape(1, slots),
        bond_column_tiles.reshape(1, slots),
        ghost_corner_lists.reshape(1, 4 * g),
        ref_pos,
        displacement,
        weighted_volume.reshape(tiles, 128),
        bond_masks,
        broken_bonds,
    )
    return force.reshape(3, points), dilatation.reshape(points)


def solution(mesh):
    in_specs = (
        P(None, ("slab", "thick")),
        P(None, ("slab", "thick")),
        P(("slab", "thick")),
        P(None, None, ("slab", "thick")),
        P(("slab", "thick")),
        P(("slab", "thick")),
        P(("slab", "thick")),
        P(("slab", "thick"), None, None),
        P(("slab", "thick"), None, None),
    )
    out_specs = (P(None, ("slab", "thick")), P(("slab", "thick")))
    return jax.shard_map(body, mesh=mesh, in_specs=in_specs, out_specs=out_specs, check_vma=False)
```

```python
import functools

import jax
import jax.numpy as jnp
from jax import lax
from jax.experimental import pallas as pl
from jax.experimental.pallas import tpu as pltpu
from jax.sharding import PartitionSpec as P

young = 25.0
poisson = 0.22
bulk_modulus = young / (3.0 * (1.0 - 2.0 * poisson))
shear_modulus = young / (2.0 * (1.0 + poisson))
volumetric_term = 3.0 * bulk_modulus - 5.0 * shear_modulus
shear_term = 15.0 * shear_modulus
floor_squared = 0.25
centre = 4.0
cycle_cells = (0, 1, 2, 3, 4, 7, 8, 11, 12, 13, 14, 15)
MESH = pl.DeviceIdType.MESH
f32, bf16 = jnp.float32, jnp.bfloat16
UNROLL = 4
NN = (((1,), (0,)), ((), ()))
NT = (((1,), (1,)), ((), ()))
TN = (((0,), (0,)), ((), ()))


def cell_plan():
    plan = []
    for cell in cycle_cells:
        row, col = cell // 4, cell % 4
        step = (-1, 0, 0, 1)
        side = (1, 0, 1, 0)
        plan.append((step[row], step[col], 2 * side[row] + side[col]))
    return plan


def dot(a, b, dims):
    return lax.dot_general(a, b, dims, preferred_element_type=f32)


def rounded(x):
    return x.astype(bf16).astype(f32)


def split3(x):
    high = rounded(x)
    rest = x - high
    middle = rounded(rest)
    return high, middle, rest - middle


def split2(x):
    high = x.astype(bf16)
    return high, (x - high.astype(f32)).astype(bf16)


def hot_dot(hot, x):
    high, middle, low = split3(x)
    return (
        dot(hot, high.astype(bf16), NN)
        + dot(hot, middle.astype(bf16), NN)
        + dot(hot, low.astype(bf16), NN)
    )


def features(payload):
    row = lax.broadcasted_iota(jnp.int32, payload.shape, 0)
    high, middle, low = split3(payload)
    square = payload * payload
    cur = jnp.sum(square[0:3], axis=0, keepdims=True)
    ref = jnp.sum(square[4:7], axis=0, keepdims=True)
    norm = jnp.where(row < 4, cur, ref)
    n_high, n_middle, n_low = split3(norm)
    which = row & 3
    norms = jnp.where(
        which == 0, n_high, jnp.where(which == 1, n_middle, jnp.where(which == 2, n_low, 0.0))
    )
    return high, middle, low, norms


def weighted_rows(payload, scale):
    row = lax.broadcasted_iota(jnp.int32, payload.shape, 0)
    both = jnp.where(row < 4, payload, scale * pltpu.roll(payload, 4, 0))
    pieces = jnp.concatenate(split3(both), axis=0).astype(bf16)
    return jnp.concatenate([pieces, pieces], axis=1)


def fold(stacked, scale):
    total = stacked[0:8] + stacked[8:16] + stacked[16:24]
    return scale * total + pltpu.roll(total, 4, 0)


def kernel(
    axes,
    row_ref,
    col_ref,
    count_ref,
    list_ref,
    row_vec,
    col_vec,
    list_vec,
    pos_hbm,
    disp_hbm,
    vol_hbm,
    mask_hbm,
    broken_hbm,
    force_ref,
    dil_ref,
    pos_ref,
    disp_ref,
    vol_ref,
    mask_ref,
    broken_ref,
    tab,
    out_buf,
    ghost_in,
    row_sum,
    col_sum,
    sum_out,
    sum_in,
    alpha_tab,
    alpha_out,
    alpha_in,
    p_high,
    p_low,
    q_row,
    q_col,
    row_force,
    col_force,
    force_out,
    force_in,
    send_sem,
    recv_sem,
    load_sem,
):
    mask_load = pltpu.make_async_copy(mask_hbm, mask_ref, load_sem.at[0])
    broken_load = pltpu.make_async_copy(broken_hbm, broken_ref, load_sem.at[1])
    point_loads = [
        pltpu.make_async_copy(pos_hbm, pos_ref, load_sem.at[2]),
        pltpu.make_async_copy(disp_hbm, disp_ref, load_sem.at[3]),
        pltpu.make_async_copy(vol_hbm, vol_ref, load_sem.at[4]),
    ]
    for load in point_loads:
        load.start()
    mask_load.start()
    broken_load.start()
    slab, thick = axes
    si, ti = lax.axis_index(slab), lax.axis_index(thick)
    n_slab, n_thick = lax.axis_size(slab), lax.axis_size(thick)
    tiles = vol_ref.shape[0]
    slots = row_vec.shape[1]
    g = list_vec.shape[1] // 4
    plan = cell_plan()

    def there(ds, dt):
        s, t = si + ds, ti + dt
        return (s >= 0) & (s < n_slab) & (t >= 0) & (t < n_thick)

    steps = [(a, b) for a in (-1, 0, 1) for b in (-1, 0, 1) if (a, b) != (0, 0)]
    barrier = pltpu.get_barrier_semaphore()
    for ds, dt in steps:

        @pl.when(there(ds, dt))
        def _(ds=ds, dt=dt):
            pl.semaphore_signal(barrier, inc=1, device_id=(si + ds, ti + dt), device_id_type=MESH)

    def copy_of(phase, q, source, target, ds, dt):
        return pltpu.make_async_remote_copy(
            src_ref=source(q),
            dst_ref=target(q),
            send_sem=send_sem.at[phase, q],
            recv_sem=recv_sem.at[phase, q],
            device_id=(si + ds, ti + dt),
            device_id_type=MESH,
        )

    def exchange(phase, source, target, sign):
        for q, (ds, dt, _c) in enumerate(plan):

            @pl.when(there(sign * ds, sign * dt))
            def _(q=q, ds=sign * ds, dt=sign * dt):
                copy_of(phase, q, source, target, ds, dt).start()

    def finish(phase, source, target, sign):
        for q, (ds, dt, _c) in enumerate(plan):

            @pl.when(there(-sign * ds, -sign * dt))
            def _(q=q, ds=-sign * ds, dt=-sign * dt):
                copy_of(phase, q, source, target, ds, dt).wait_recv()

            @pl.when(there(sign * ds, sign * dt))
            def _(q=q, ds=sign * ds, dt=sign * dt):
                copy_of(phase, q, source, target, ds, dt).wait_send()

    for q, (ds, dt, _c) in enumerate(plan):

        @pl.when(jnp.logical_not(there(ds, dt)))
        def _(q=q):
            ghost_in[q * g : (q + 1) * g] = jnp.zeros((g, 8, 128), f32)
            alpha_in[q * g : (q + 1) * g] = jnp.zeros((g, 128), f32)

        @pl.when(jnp.logical_not(there(-ds, -dt)))
        def _(q=q):
            sum_in[q] = jnp.zeros((g, 128), f32)
            force_in[q] = jnp.zeros((g, 384), f32)

    def build(t, carry):
        at = pl.ds(pl.multiple_of(t * 128, 128), 128)
        ref = pos_ref[:, at] - centre
        tab[t] = jnp.concatenate(
            [
                ref + disp_ref[:, at],
                jnp.ones((1, 128), f32),
                ref,
                shear_term / vol_ref[pl.ds(t, 1), :],
            ],
            axis=0,
        )
        return carry

    for load in point_loads:
        load.wait()
    lax.fori_loop(0, tiles, build, 0, unroll=4)

    for s in range(2):
        for t in range(2):

            def pick(i, carry, s=s, t=t):
                out_buf[(2 * s + t) * g + i] = tab[list_ref[s, t, i]]
                return carry

            lax.fori_loop(0, g, pick, 0, unroll=4)

    peers = sum(there(ds, dt).astype(jnp.int32) for ds, dt in steps)
    pl.semaphore_wait(barrier, peers)

    corner = [c for _s, _t, c in plan]
    payload = (
        0,
        lambda q: out_buf.at[corner[q] * g : (corner[q] + 1) * g],
        lambda q: ghost_in.at[q * g : (q + 1) * g],
        -1,
    )
    exchange(*payload)
    finish(*payload)
    tab[tiles:] = ghost_in[...]
    mask_load.wait()
    broken_load.wait()

    sub = lax.broadcasted_iota(jnp.int32, (8, 128), 0)
    cur_rows = (sub < 3).astype(f32)
    ref_rows = ((sub >= 4) & (sub < 7)).astype(f32)
    one8 = jnp.ones((8, 128), f32)
    ones = jnp.ones((8, 256), bf16)
    word = lax.broadcasted_iota(jnp.int32, (16, 128), 0)
    lane = lax.broadcasted_iota(jnp.int32, (16, 128), 1)
    triangle = (1 << jnp.clip(lane - 8 * word, 0, 8)) - 1
    bit = lax.broadcasted_iota(jnp.int32, (16, 8, 128), 1)
    live = count_ref[0]

    def first(k):
        a, b = row_ref[k], col_ref[k]
        vi, vj = tab[a], tab[b]
        hi, mi, li, ni = features(vi)
        hj, mj, lj, nj = features(vj)
        left = jnp.concatenate([hi, hi, mi, mi, hi, li, ni, one8], axis=0).astype(bf16)
        hj, mj, lj = -2.0 * hj, -2.0 * mj, -2.0 * lj
        base = (hj, mj, hj, mj, lj, hj, one8, nj)
        right = jnp.concatenate(
            [
                jnp.concatenate([x * ref_rows for x in base], axis=0),
                jnp.concatenate([x * cur_rows for x in base], axis=0),
            ],
            axis=1,
        ).astype(bf16)
        squares = jnp.maximum(dot(left, right, TN), floor_squared)
        ref_sq, cur_sq = squares[:, 0:128], squares[:, 128:256]
        ref_inv, cur_inv = lax.rsqrt(ref_sq), lax.rsqrt(cur_sq)
        words = mask_ref[k] & ~broken_ref[k]
        words = words & jnp.where(a == b, triangle, 255)
        words = words & jnp.where(k < live, 255, 0)
        spread = jnp.broadcast_to(words[:, None, :], (16, 8, 128))
        keep = ((spread & (1 << bit)) != 0).reshape(128, 128)
        e = jnp.where(keep, cur_sq * cur_inv - ref_sq * ref_inv, 0.0)
        p = jnp.where(keep, cur_inv, 0.0)
        q = jnp.where(keep, ref_inv - cur_inv, 0.0)
        col_sum[pl.ds(k, 1), :] = jnp.sum(e, axis=0, keepdims=True)
        row_sum[pl.ds(k, 1), :] = dot(ones, jnp.concatenate(split2(e), axis=1), NT)[0:1]
        ph, plow = split2(p)
        p_high[k] = ph
        p_low[k] = plow
        qh, qlow = split2(q)
        gi, gj = vi[7:8], vj[7:8]
        q_row[k] = fold(
            dot(weighted_rows(vj, gj), jnp.concatenate([qh, qlow], axis=1), NT), gi
        )
        q_col[k] = fold(
            dot(weighted_rows(vi, gi), jnp.concatenate([qh, qlow], axis=0), NN), gj
        )

    def first_loop(block, carry):
        for u in range(UNROLL):
            first(block * UNROLL + u)
        return carry

    lax.fori_loop(0, slots // UNROLL, first_loop, 0)

    row_hot = (
        lax.broadcasted_iota(jnp.int32, (tiles, slots), 0) == row_vec[...]
    ).astype(f32).astype(bf16)
    col_hot = (
        lax.broadcasted_iota(jnp.int32, (tiles + 12 * g, slots), 0) == col_vec[...]
    ).astype(f32).astype(bf16)
    box_hot = (
        lax.broadcasted_iota(jnp.int32, (tiles, 4 * g), 0) == list_vec[...]
    ).astype(f32).astype(bf16)

    def returned(buffer):
        corners = []
        for c in range(4):
            parts = [buffer[q] for q in range(12) if corner[q] == c]
            corners.append(parts[0] + parts[1] + parts[2])
        return hot_dot(box_hot, jnp.concatenate(corners, axis=0))

    col_part = hot_dot(col_hot, col_sum[...])
    sum_out[...] = col_part[tiles:]
    sums = (1, lambda q: sum_out.at[q * g : (q + 1) * g], lambda q: sum_in.at[q], 1)
    exchange(*sums)
    own = hot_dot(row_hot, row_sum[...]) + col_part[:tiles]
    finish(*sums)
    volume = vol_ref[...]
    dilatation = 3.0 * (own + returned(sum_in)) / volume
    dil_ref[...] = dilatation
    alpha_tab[0:tiles] = volumetric_term * dilatation / volume

    for s in range(2):
        for t in range(2):

            def pick_alpha(i, carry, s=s, t=t):
                alpha_out[pl.ds((2 * s + t) * g + i, 1), :] = alpha_tab[
                    pl.ds(list_ref[s, t, i], 1), :
                ]
                return carry

            lax.fori_loop(0, g, pick_alpha, 0, unroll=4)

    alphas = (
        2,
        lambda q: alpha_out.at[corner[q] * g : (corner[q] + 1) * g],
        lambda q: alpha_in.at[q * g : (q + 1) * g],
        -1,
    )
    exchange(*alphas)
    finish(*alphas)
    alpha_tab[tiles:] = alpha_in[...]

    def second(k):
        a, b = row_ref[k], col_ref[k]
        vi, vj = tab[a], tab[b]
        ai, aj = alpha_tab[pl.ds(a, 1), :], alpha_tab[pl.ds(b, 1), :]
        ph, plow = p_high[k], p_low[k]
        rows = q_row[k] + fold(
            dot(weighted_rows(vj, aj), jnp.concatenate([ph, plow], axis=1), NT), ai
        )
        cols = q_col[k] + fold(
            dot(weighted_rows(vi, ai), jnp.concatenate([ph, plow], axis=0), NN), aj
        )
        rows = rows - vi * rows[3:4]
        cols = cols - vj * cols[3:4]
        for c in range(3):
            row_force[c, pl.ds(k, 1), :] = rows[c : c + 1]
            col_force[c, pl.ds(k, 1), :] = cols[c : c + 1]

    def second_loop(block, carry):
        for u in range(2 * UNROLL):
            second(block * 2 * UNROLL + u)
        return carry

    lax.fori_loop(0, slots // (2 * UNROLL), second_loop, 0)

    col_part = hot_dot(col_hot, jnp.concatenate([col_force[c] for c in range(3)], axis=1))
    force_out[...] = col_part[tiles:]
    forces = (3, lambda q: force_out.at[q * g : (q + 1) * g], lambda q: force_in.at[q], 1)
    exchange(*forces)
    own = hot_dot(row_hot, jnp.concatenate([row_force[c] for c in range(3)], axis=1)) + col_part[:tiles]
    finish(*forces)
    total = own + returned(force_in)
    for c in range(3):
        force_ref[c] = total[:, c * 128 : (c + 1) * 128]


def body(
    ref_pos,
    displacement,
    weighted_volume,
    ghost_corner_lists,
    bond_row_tiles,
    bond_column_tiles,
    bond_count,
    bond_masks,
    broken_bonds,
):
    points = ref_pos.shape[1]
    tiles = points // 128
    g = ghost_corner_lists.shape[2]
    slots = bond_row_tiles.shape[0]
    smem = pl.BlockSpec(memory_space=pltpu.SMEM)
    vmem = pl.BlockSpec(memory_space=pltpu.VMEM)
    force, dilatation = pl.pallas_call(
        functools.partial(kernel, ("slab", "thick")),
        out_shape=(
            jax.ShapeDtypeStruct((3, tiles, 128), f32),
            jax.ShapeDtypeStruct((tiles, 128), f32),
        ),
        in_specs=[smem] * 4 + [vmem] * 3 + [pl.BlockSpec(memory_space=pltpu.HBM)] * 5,
        out_specs=(vmem, vmem),
        scratch_shapes=[
            pltpu.VMEM(ref_pos.shape, f32),
            pltpu.VMEM(displacement.shape, f32),
            pltpu.VMEM((tiles, 128), f32),
            pltpu.VMEM(bond_masks.shape, jnp.int32),
            pltpu.VMEM(bond_masks.shape, jnp.int32),
            pltpu.VMEM((tiles + 12 * g, 8, 128), f32),
            pltpu.VMEM((4 * g, 8, 128), f32),
            pltpu.VMEM((12 * g, 8, 128), f32),
            pltpu.VMEM((slots, 128), f32),
            pltpu.VMEM((slots, 128), f32),
            pltpu.VMEM((12 * g, 128), f32),
            pltpu.VMEM((12, g, 128), f32),
            pltpu.VMEM((tiles + 12 * g, 128), f32),
            pltpu.VMEM((4 * g, 128), f32),
            pltpu.VMEM((12 * g, 128), f32),
            pltpu.VMEM((slots, 128, 128), bf16),
            pltpu.VMEM((slots, 128, 128), bf16),
            pltpu.VMEM((slots, 8, 128), f32),
            pltpu.VMEM((slots, 8, 128), f32),
            pltpu.VMEM((3, slots, 128), f32),
            pltpu.VMEM((3, slots, 128), f32),
            pltpu.VMEM((12 * g, 384), f32),
            pltpu.VMEM((12, g, 384), f32),
            pltpu.SemaphoreType.DMA((4, 12)),
            pltpu.SemaphoreType.DMA((4, 12)),
            pltpu.SemaphoreType.DMA((5,)),
        ],
        compiler_params=pltpu.CompilerParams(
            collective_id=0, has_side_effects=True, vmem_limit_bytes=40 * 1024 * 1024
        ),
    )(
        bond_row_tiles,
        bond_column_tiles,
        bond_count,
        ghost_corner_lists,
        bond_row_tiles.reshape(1, slots),
        bond_column_tiles.reshape(1, slots),
        ghost_corner_lists.reshape(1, 4 * g),
        ref_pos,
        displacement,
        weighted_volume.reshape(tiles, 128),
        bond_masks,
        broken_bonds,
    )
    return force.reshape(3, points), dilatation.reshape(points)


def solution(mesh):
    in_specs = (
        P(None, ("slab", "thick")),
        P(None, ("slab", "thick")),
        P(("slab", "thick")),
        P(None, None, ("slab", "thick")),
        P(("slab", "thick")),
        P(("slab", "thick")),
        P(("slab", "thick")),
        P(("slab", "thick"), None, None),
        P(("slab", "thick"), None, None),
    )
    out_specs = (P(None, ("slab", "thick")), P(("slab", "thick")))
    return jax.shard_map(body, mesh=mesh, in_specs=in_specs, out_specs=out_specs, check_vma=False)
```
